256 devices in a mesh: row: 8 (over y, core), col: 32 (over z, x).
Axes of the slice: x: 4, y: 4, z: 8, core: 2. Of those that a mesh axis runs over, the one named last changes fastest.
Arguments:
- amplitudes: float32 [320, 102400], P('col', 'row'), may hold values from -6 to 6
- integral: float32 [20480, 25600], P('col', 'row'), may hold values from -0.0390625 to 0.0390625
- residual_in: float32 [1280, 20480], P('col', 'row'), may hold values from -6 to 6
Outputs:
- residual_out: float32 [1280, 20480], P('col', 'row')
The draws below stay inside these ranges and needn't reach their ends.
All inputs are finite; a program needn't handle non-finite values.
Results may differ from the reference program's by a relative error of at most 0.00005.
Values sent between devices are 32-bit elements; how exact they have to be, the bound alone decides.
No kernel may reach another device: no remote copies, remote signals or barrier semaphores. Data moves between devices by JAX's collectives and lax.ppermute only.
A program may use at most 256 MiB of HBM per device.

```python
import jax
import jax.numpy as jnp
from jax import lax

O = 80
V = 320
NI = 4
NJ = 64


def levels(own_key, extent, shards, smallest, top_value):
    gain, own = 1.0, jax.random.fold_in(own_key, 6)
    for axis_at, blocks in shards:
        heights = jnp.exp(jax.random.uniform(jax.random.fold_in(own, axis_at), (blocks,), jnp.float32, smallest / len(shards), top_value / len(shards)))
        gain = gain * jnp.repeat(heights, extent[axis_at] // blocks).reshape([-1 if axis == axis_at else 1 for axis in range(len(extent))])
    return gain


def bell_draw(key, dims, width, most, cuts=(), kind=jnp.bfloat16):
    loudness = levels(key, dims, cuts, -0.22, 0.18) if cuts else 1.0
    entries = jax.random.normal(key, dims, jnp.float32) * width * loudness
    return jnp.minimum(jnp.maximum(entries, -most), most).astype(kind)


def setup_inputs(seed: int = 0) -> dict:
    seeds = jax.random.split(jax.random.key(seed), 4)
    amplitudes = bell_draw(seeds[0], (V, O * NI * V), 1.0, 6.0, ((0, 32), (1, 8)), jnp.float32)
    integral = bell_draw(seeds[1], (V * NJ, O * V), (O * V) ** -0.5, 0.0390625, ((0, 32), (1, 8)), jnp.float32)
    residual_in = bell_draw(seeds[2], (V * NI, NJ * V), 1.0, 6.0, ((0, 32), (1, 8)), jnp.float32)
    return dict(amplitudes=amplitudes, integral=integral, residual_in=residual_in)


def reference(amplitudes, integral, residual_in):
    amp_matrix = amplitudes.reshape(V, O, NI * V).transpose(1, 0, 2).reshape(O * V, NI * V)
    cycle_term = jnp.dot(integral, amp_matrix, precision=lax.Precision.HIGHEST, preferred_element_type=jnp.float32)
    cycle_term = cycle_term.reshape(V, NJ, NI, V).transpose(0, 2, 1, 3).reshape(V * NI, NJ * V)
    return residual_in + cycle_term
```

```python
import functools

import jax
import jax.numpy as jnp
from jax import lax
from jax.experimental import pallas as pl
from jax.experimental.pallas import tpu as pltpu
from jax.sharding import PartitionSpec as P

O = 80
V = 320
NI = 4
NJ = 64
LANES = 128
TILES = 2


def split(x):
    high = x.astype(jnp.bfloat16)
    return high, (x - high.astype(jnp.float32)).astype(jnp.bfloat16)


def product_kernel(k_local, right_ref, left_ref, out_ref, left_high, left_low, right_high, right_low):
    @pl.when(pl.program_id(0) == 0)
    def _():
        high, low = split(left_ref[...])
        left_high[...] = high
        left_low[...] = low

    rows = right_ref.reshape(right_ref.shape[0] * right_ref.shape[2], LANES)
    stride = k_local * TILES
    for k in range(k_local):
        for t in range(TILES):
            high, low = split(rows[pl.ds(k * TILES + t, V, stride=stride), :])
            right_high[k * V : (k + 1) * V, t * LANES : (t + 1) * LANES] = high
            right_low[k * V : (k + 1) * V, t * LANES : (t + 1) * LANES] = low
    dot = functools.partial(jnp.dot, preferred_element_type=jnp.float32)
    total = dot(left_high[...], right_high[...])
    total += dot(left_high[...], right_low[...])
    total += dot(left_low[...], right_high[...])
    groups, b_local = out_ref.shape[0], out_ref.shape[1]
    total = total.reshape(b_local, groups, NJ // groups, TILES * LANES)
    for group in range(groups):
        out_ref[group] = total[:, group]


def product(right, left, k_local, b_local, groups):
    shards, chunks, rows, _ = right.shape
    width = TILES * LANES
    return pl.pallas_call(
        functools.partial(product_kernel, k_local),
        grid=(chunks,),
        in_specs=[
            pl.BlockSpec((shards, 1, rows, LANES), lambda n: (0, n, 0, 0)),
            pl.BlockSpec(left.shape, lambda n: (0, 0), pipeline_mode=pl.Buffered(1)),
        ],
        out_specs=pl.BlockSpec((groups, b_local, NJ // groups, width), lambda n: (0, 0, 0, n)),
        out_shape=jax.ShapeDtypeStruct((groups, b_local, NJ // groups, chunks * width), jnp.float32),
        scratch_shapes=[
            pltpu.VMEM(left.shape, jnp.bfloat16),
            pltpu.VMEM(left.shape, jnp.bfloat16),
            pltpu.VMEM((left.shape[1], width), jnp.bfloat16),
            pltpu.VMEM((left.shape[1], width), jnp.bfloat16),
        ],
        compiler_params=pltpu.CompilerParams(vmem_limit_bytes=56 * 1024 * 1024),
    )(right, left)


def per_device(amplitudes, integral, residual_in):
    groups = lax.axis_size("row")
    shards = lax.axis_size("col")
    k_local = O // groups
    b_local = integral.shape[0] // NJ
    c_local = amplitudes.shape[0]
    chunks = NI * V // (TILES * LANES)
    rows = c_local * k_local * TILES
    own = amplitudes.reshape(c_local * k_local, chunks, TILES * LANES).transpose(1, 0, 2)
    piece = lax.all_gather(own.reshape(chunks * rows, LANES), "col", axis=0, tiled=True)
    term = product(piece.reshape(shards, chunks, rows, LANES), integral, k_local, b_local, groups)
    block = lax.psum_scatter(term, "row", scatter_dimension=0, tiled=True)
    block = block.reshape(b_local, NJ // groups, NI, V).transpose(0, 2, 1, 3)
    return residual_in + block.reshape(residual_in.shape)


def solution(mesh):
    return jax.shard_map(
        per_device,
        mesh=mesh,
        in_specs=(P("col", "row"), P("col", "row"), P("col", "row")),
        out_specs=P("col", "row"),
        check_vma=False,
    )
```

```python
import functools

import jax
import jax.numpy as jnp
from jax import lax
from jax.experimental import pallas as pl
from jax.experimental.pallas import tpu as pltpu
from jax.sharding import PartitionSpec as P

O = 80
V = 320
NI = 4
NJ = 64
LANES = 128
X, Y, Z, CORES = 4, 4, 8, 2
PLAN = (2, 2, 2, 2, 2)

ARRANGE = 160
BLOCK = 320
LIMIT1, LIMIT2 = 56, 32

dot = functools.partial(jnp.dot, preferred_element_type=jnp.float32)


def split(x):
    high = x.astype(jnp.bfloat16)
    return high, (x - high.astype(jnp.float32)).astype(jnp.bfloat16)


def mate(place, core):
    return (place + 1 - 2 * ((place + core) % 2)) % 4


def links(target):
    pairs = []
    for y in range(Y):
        for core in range(CORES):
            for z in range(Z):
                for x in range(X):
                    to_x, to_y, to_z, to_core = target(x, y, z, core)
                    here = ((y * CORES + core) * Z + z) * X + x
                    there = ((to_y * CORES + to_core) * Z + to_z % Z) * X + to_x
                    pairs.append((here, there))
    return pairs


def send(value, target):
    return lax.ppermute(value, ("row", "col"), links(target))


def to_x_mate(x, y, z, c):
    return mate(x, c), y, z, c


def to_x_mate_crossed(x, y, z, c):
    return mate(x, c), y, z, 1 - c


def to_x_other(x, y, z, c):
    return mate(x, 1 - c), y, z, c


def to_y_mate(x, y, z, c):
    return x, mate(y, c), z, c


def to_y_other(x, y, z, c):
    return x, mate(y, 1 - c), z, c


def to_core(x, y, z, c):
    return x, y, z, 1 - c


def up(x, y, z, c):
    return x, y, z + 1, c


def down(x, y, z, c):
    return x, y, z - 1, c


def after(value, *others):
    return lax.optimization_barrier((value, *others))[0]


def turn(k_local, source_ref, left_ref):
    wanted = source_ref.shape[1]
    order = lax.broadcasted_iota(jnp.int32, (V, wanted), 0) == source_ref[...]
    rows = left_ref.shape[0]
    parts = [part[:, k * V : (k + 1) * V] for part in split(left_ref[...]) for k in range(k_local)]
    turned = dot(jnp.concatenate(parts, axis=0), order.astype(jnp.float32).astype(jnp.bfloat16))
    turned = [turned[n * rows : (n + 1) * rows] for n in range(2 * k_local)]
    return turned[:k_local], turned[k_local:]


def keep_kernel(k_local, source_ref, left_ref, high_ref, low_ref):
    high, low = turn(k_local, source_ref, left_ref)
    high_ref[...] = jnp.concatenate(high, axis=1).astype(jnp.bfloat16)
    low_ref[...] = jnp.concatenate(low, axis=1).astype(jnp.bfloat16)


def away_kernel(k_local, source_ref, left_ref, send_ref):
    rows = left_ref.shape[0]
    high, low = turn(k_local, source_ref, left_ref)
    away = jnp.concatenate([a + b for a, b in zip(high, low)], axis=1)
    full = away.shape[1] // LANES
    for t in range(full):
        send_ref[t * rows : (t + 1) * rows, :] = away[:, t * LANES : (t + 1) * LANES]
    rest = away[:, full * LANES :]
    send_ref[full * rows :, :] = jnp.concatenate([rest[: rows // 2], rest[rows // 2 :]], axis=1)


def arrange(kernel, left, source, k_local, blocks, dtype):
    rows, depth = left.shape
    block = ARRANGE
    return pl.pallas_call(
        functools.partial(kernel, k_local),
        grid=(rows // block,),
        in_specs=[pl.BlockSpec(source.shape, lambda m: (0, 0)), pl.BlockSpec((block, depth), lambda m: (m, 0))],
        out_specs=[pl.BlockSpec(shape, lambda m: (m, 0)) for shape in blocks],
        out_shape=[jax.ShapeDtypeStruct((shape[0] * (rows // block), shape[1]), dtype) for shape in blocks],
        compiler_params=pltpu.CompilerParams(vmem_limit_bytes=LIMIT1 * 1024 * 1024),
        cost_estimate=pl.CostEstimate(flops=rows * depth * V * 2, bytes_accessed=rows * depth * 6, transcendentals=0),
    )(source, left)


def product_kernel(k_local, tiles, ringed, place_ref, *refs):
    *pieces, high_ref, low_ref, got_ref, keep_ref, send_ref, right_high, right_low, total_ref = refs
    shared = Z * O // 8
    size = O // 8 * k_local * tiles

    @pl.when(pl.program_id(0) == 0)
    def _():
        if ringed:
            own, other = pieces
            own, other = own.reshape(Z * size, LANES), other
            starts = ((own, 0, size), (other, 0, size))
        else:
            (rows_ref,) = pieces
            starts = ((rows_ref, 0, 2 * size), (rows_ref, size, 2 * size))
        for k in range(k_local):
            for t in range(tiles):
                for half, (ref, start, step) in enumerate(starts):
                    first = start + k * tiles + t
                    if step == size:
                        block = ref[pl.ds(first, shared, stride=k_local * tiles), :]
                    else:
                        block = jnp.concatenate(
                            [ref[pl.ds(first + z * step, O // 8, stride=k_local * tiles), :] for z in range(Z)]
                        )
                    high, low = split(block)
                    at = (2 * k + half) * shared
                    right_high[at : at + shared, t * LANES : (t + 1) * LANES] = high
                    right_low[at : at + shared, t * LANES : (t + 1) * LANES] = low

    rows, depth = high_ref.shape
    full = depth // LANES
    got = []
    for at in range(0, rows * depth // LANES, ARRANGE * depth // LANES):
        blocks = [got_ref[at + t * ARRANGE : at + (t + 1) * ARRANGE, :] for t in range(full)]
        rest = got_ref[at + full * ARRANGE : at + ARRANGE * depth // LANES, :]
        blocks.append(jnp.concatenate([rest[:, : LANES // 2], rest[:, LANES // 2 :]], axis=0))
        got.append(jnp.concatenate(blocks, axis=1))
    got_high, got_low = split(jnp.concatenate(got, axis=0))
    for at, (high, low) in enumerate(((high_ref[...], low_ref[...]), (got_high, got_low))):
        total_ref[...] = dot(high, right_high[...]) + dot(high, right_low[...]) + dot(low, right_high[...])
        for b in range(rows // NJ):
            for out, slots in ((keep_ref, (0, 1)), (send_ref, (2, 3))):
                for slot, which in enumerate(slots):
                    for part in range(CORES):
                        start = pl.multiple_of(b * NJ + place_ref[which * CORES + part] * 8, 8)
                        out[slot, at, b, part * 8 : (part + 1) * 8, :] = total_ref[pl.ds(start, 8), :]


def product(pieces, at, high, low, got, place, k_local, tiles):
    rows, depth = high.shape
    width = tiles * LANES
    block = BLOCK
    b_local = rows // NJ
    ringed = len(pieces) == 2
    left = pl.BlockSpec((block, depth), lambda m, s: (m, 0))
    specs = [pl.BlockSpec(piece.shape, lambda m, s: (0, 0)) for piece in pieces]
    if ringed:
        specs[0] = pl.BlockSpec((Z, 1) + pieces[0].shape[2:], lambda m, s: (0, at, 0, 0))
    away = pl.BlockSpec((block * depth // LANES, LANES), lambda m, s: (m, 0))
    out = pl.BlockSpec((2, 2, block // NJ, 16, width), lambda m, s: (0, 0, m, 0, 0))
    shape = jax.ShapeDtypeStruct((2, 2, b_local, 16, width), jnp.float32)
    return pl.pallas_call(
        functools.partial(product_kernel, k_local, tiles, ringed),
        grid_spec=pltpu.PrefetchScalarGridSpec(
            num_scalar_prefetch=1,
            grid=(rows // block,),
            in_specs=specs + [left, left, away],
            out_specs=[out, out],
            scratch_shapes=[
                pltpu.VMEM((depth, width), jnp.bfloat16),
                pltpu.VMEM((depth, width), jnp.bfloat16),
                pltpu.VMEM((block, width), jnp.float32),
            ],
        ),
        out_shape=[shape, shape],
        compiler_params=pltpu.CompilerParams(vmem_limit_bytes=LIMIT2 * 1024 * 1024),
        cost_estimate=pl.CostEstimate(
            flops=rows * depth * width * 12, bytes_accessed=rows * depth * 12 + rows * width * 16, transcendentals=0
        ),
    )(place, *pieces, high, low, got)


def per_device(amplitudes, integral, residual_in):
    row, col = lax.axis_index("row"), lax.axis_index("col")
    y, core, z, x = row // CORES, row % CORES, col // X, col % X
    k_local = O // lax.axis_size("row")
    c_local = amplitudes.shape[0]
    b_local = integral.shape[0] // NJ

    x_mate, x_other = mate(x, core), mate(x, 1 - core)
    xs = jnp.stack([x, x_other, x_mate, mate(x_mate, 1 - core)])
    zs = jnp.arange(Z)
    source = (zs[None, :, None] * X + xs[:, None, None]) * c_local + jnp.arange(c_local)[None, None, :]
    source = source.reshape(1, V).astype(jnp.int32)
    y_mate, y_other = mate(y, core), mate(y, 1 - core)
    ys = jnp.stack([y, y_other, y_mate, mate(y_mate, 1 - core)])
    place = (ys[:, None] * CORES + jnp.stack([core, 1 - core])[None, :]).reshape(8)
    place = jnp.concatenate([place, z[None]]).astype(jnp.int32)

    blocks, at = [], 0
    for tiles in PLAN:
        part = amplitudes.reshape(c_local * k_local, NI * V)[:, at * LANES : (at + tiles) * LANES]
        blocks.append(part.reshape(c_local * k_local * tiles, LANES))
        at += tiles
    lead, rest = blocks[0], blocks[1:]
    groups = [[q * X + r for q in range(Z)] for r in range(X)]
    gather = functools.partial(lax.all_gather, axis_name="col", axis=0, tiled=True, axis_index_groups=groups)
    gathered = gather(jnp.concatenate(rest)).reshape(Z, -1, LANES)
    pair = jnp.concatenate([lead, send(lead, to_x_other)])
    paired = gather(pair)
    half = V // 2
    packed = (ARRANGE * k_local * half // LANES, LANES)
    (away,) = arrange(away_kernel, integral, source[:, half:], k_local, [packed], jnp.float32)
    got = send(away, to_x_mate)
    natural = (ARRANGE, k_local * half)
    high, low = arrange(keep_kernel, integral, after(source[:, :half], away, pair), k_local, [natural] * 2, jnp.bfloat16)
    gathered = after(gathered, high)
    pieces, at = [], 0
    for block in rest:
        own = gathered[:, at : at + block.shape[0]]
        at += block.shape[0]
        pieces.append([own[:, None], send(own.reshape(-1, LANES), to_x_other)])
    pieces.append([paired])
    plan = PLAN[1:] + PLAN[:1]

    count = len(plan)
    keeps, gives, firsts, seconds = [], [], [], []
    for n in range(count + 2):
        if n < count:
            if n >= 2:
                place = after(place, firsts[n - 2])
            if n >= 3:
                place = after(place, seconds[n - 3])
            keep, give = product(pieces[n], 0, high, low, got, place, k_local, plan[n])
            place = after(place, keep)
            keeps.append(keep)
            gives.append(send(give, to_y_mate))
        if 0 <= n - 1 < count:
            mine = after(keeps[n - 1], keeps[n]) if n < count else keeps[n - 1]
            firsts.append(mine + gives[n - 1])
        if 0 <= n - 2 < count:
            mine = after(firsts[n - 2], keeps[n]) if n < count else firsts[n - 2]
            seconds.append(mine[0] + send(firsts[n - 2][1], to_y_other))
    results = []
    for group in (seconds[:3], seconds[3:]):
        second = jnp.concatenate(group, axis=-1)
        own, mates = second[0], second[1]
        total = own[:, :8] + send(own[:, 8:], to_core)
        total += send(mates[:, :8], to_x_mate)
        total += send(mates[:, 8:], to_x_mate_crossed)
        results.append(total)
    block = jnp.concatenate(results, axis=-1)
    first = PLAN[0] * LANES
    block = jnp.concatenate([block[..., -first:], block[..., :-first]], axis=-1)
    block = block.reshape(b_local, 8, NI, V).transpose(0, 2, 1, 3)
    return residual_in + block.reshape(residual_in.shape)


def solution(mesh):
    return jax.shard_map(
        per_device,
        mesh=mesh,
        in_specs=(P("col", "row"), P("col", "row"), P("col", "row")),
        out_specs=P("col", "row"),
        check_vma=False,
    )
```

```python
import functools

import jax
import jax.numpy as jnp
from jax import lax
from jax.experimental import pallas as pl
from jax.experimental.pallas import tpu as pltpu
from jax.sharding import PartitionSpec as P

O = 80
V = 320
NI = 4
NJ = 64
LANES = 128
X, Y, Z, CORES = 4, 4, 8, 2
PLAN = (2, 2, 2, 2, 2)

ARRANGE = 320
BLOCK = 320
LAST = 2
LIMIT1, LIMIT2 = 56, 32

dot = functools.partial(jnp.dot, preferred_element_type=jnp.float32)


def split(x):
    high = x.astype(jnp.bfloat16)
    return high, (x - high.astype(jnp.float32)).astype(jnp.bfloat16)


def mate(place, core):
    return (place + 1 - 2 * ((place + core) % 2)) % 4


def links(target):
    pairs = []
    for y in range(Y):
        for core in range(CORES):
            for z in range(Z):
                for x in range(X):
                    to_x, to_y, to_z, to_core = target(x, y, z, core)
                    here = ((y * CORES + core) * Z + z) * X + x
                    there = ((to_y * CORES + to_core) * Z + to_z % Z) * X + to_x
                    pairs.append((here, there))
    return pairs


def send(value, target):
    return lax.ppermute(value, ("row", "col"), links(target))


def to_x_mate(x, y, z, c):
    return mate(x, c), y, z, c


def to_x_mate_crossed(x, y, z, c):
    return mate(x, c), y, z, 1 - c


def to_x_other(x, y, z, c):
    return mate(x, 1 - c), y, z, c


def to_y_mate(x, y, z, c):
    return x, mate(y, c), z, c


def to_y_other(x, y, z, c):
    return x, mate(y, 1 - c), z, c


def to_y_other_crossed(x, y, z, c):
    return x, mate(y, 1 - c), z, 1 - c


def to_corner(x, y, z, c):
    return mate(x, c), mate(y, 1 - c), z, c


def to_corner_crossed(x, y, z, c):
    return mate(x, c), mate(y, 1 - c), z, 1 - c


def to_core(x, y, z, c):
    return x, y, z, 1 - c


def up(x, y, z, c):
    return x, y, z + 1, c


def down(x, y, z, c):
    return x, y, z - 1, c


def after(value, *others):
    return lax.optimization_barrier((value, *others))[0]


def turn(k_local, source_ref, left_ref):
    wanted = source_ref.shape[1]
    order = lax.broadcasted_iota(jnp.int32, (V, wanted), 0) == source_ref[...]
    rows = left_ref.shape[0]
    parts = [part[:, k * V : (k + 1) * V] for part in split(left_ref[...]) for k in range(k_local)]
    turned = dot(jnp.concatenate(parts, axis=0), order.astype(jnp.float32).astype(jnp.bfloat16))
    turned = [turned[n * rows : (n + 1) * rows] for n in range(2 * k_local)]
    return turned[:k_local], turned[k_local:]


def keep_kernel(k_local, source_ref, left_ref, high_ref, low_ref):
    high, low = turn(k_local, source_ref, left_ref)
    high_ref[...] = jnp.concatenate(high, axis=1).astype(jnp.bfloat16)
    low_ref[...] = jnp.concatenate(low, axis=1).astype(jnp.bfloat16)


def away_kernel(k_local, source_ref, left_ref, send_ref):
    rows = left_ref.shape[0]
    high, low = turn(k_local, source_ref, left_ref)
    away = jnp.concatenate([a + b for a, b in zip(high, low)], axis=1)
    full = away.shape[1] // LANES
    for t in range(full):
        send_ref[t * rows : (t + 1) * rows, :] = away[:, t * LANES : (t + 1) * LANES]
    rest = away[:, full * LANES :]
    send_ref[full * rows :, :] = jnp.concatenate([rest[: rows // 2], rest[rows // 2 :]], axis=1)


def arrange(kernel, left, source, k_local, blocks, dtype):
    rows, depth = left.shape
    block = ARRANGE
    return pl.pallas_call(
        functools.partial(kernel, k_local),
        grid=(rows // block,),
        in_specs=[pl.BlockSpec(source.shape, lambda m: (0, 0)), pl.BlockSpec((block, depth), lambda m: (m, 0))],
        out_specs=[pl.BlockSpec(shape, lambda m: (m, 0)) for shape in blocks],
        out_shape=[jax.ShapeDtypeStruct((shape[0] * (rows // block), shape[1]), dtype) for shape in blocks],
        compiler_params=pltpu.CompilerParams(vmem_limit_bytes=LIMIT1 * 1024 * 1024),
        cost_estimate=pl.CostEstimate(flops=rows * depth * V * 2, bytes_accessed=rows * depth * 6, transcendentals=0),
    )(source, left)


def product_kernel(k_local, tiles, ringed, place_ref, *refs):
    *pieces, high_ref, low_ref, got_ref, keep_ref, send_ref, right_high, right_low, total_ref = refs
    shared = Z * O // 8
    size = O // 8 * k_local * tiles

    @pl.when(pl.program_id(0) == 0)
    def _():
        if ringed:
            own, other = pieces
            own, other = own.reshape(Z * size, LANES), other
            starts = ((own, 0, size), (other, 0, size))
        else:
            (rows_ref,) = pieces
            starts = ((rows_ref, 0, 2 * size), (rows_ref, size, 2 * size))
        for k in range(k_local):
            for t in range(tiles):
                for half, (ref, start, step) in enumerate(starts):
                    first = start + k * tiles + t
                    if step == size:
                        block = ref[pl.ds(first, shared, stride=k_local * tiles), :]
                    else:
                        block = jnp.concatenate(
                            [ref[pl.ds(first + z * step, O // 8, stride=k_local * tiles), :] for z in range(Z)]
                        )
                    high, low = split(block)
                    at = (2 * k + half) * shared
                    right_high[at : at + shared, t * LANES : (t + 1) * LANES] = high
                    right_low[at : at + shared, t * LANES : (t + 1) * LANES] = low

    rows, depth = high_ref.shape
    full = depth // LANES
    got = []
    for at in range(0, rows * depth // LANES, ARRANGE * depth // LANES):
        blocks = [got_ref[at + t * ARRANGE : at + (t + 1) * ARRANGE, :] for t in range(full)]
        rest = got_ref[at + full * ARRANGE : at + ARRANGE * depth // LANES, :]
        blocks.append(jnp.concatenate([rest[:, : LANES // 2], rest[:, LANES // 2 :]], axis=0))
        got.append(jnp.concatenate(blocks, axis=1))
    got_high, got_low = split(jnp.concatenate(got, axis=0))
    for at, (high, low) in enumerate(((high_ref[...], low_ref[...]), (got_high, got_low))):
        total_ref[...] = dot(high, right_high[...]) + dot(high, right_low[...]) + dot(low, right_high[...])
        for b in range(rows // NJ):
            for out, slots in ((keep_ref, (0, 1)), (send_ref, (2, 3))):
                for slot, which in enumerate(slots):
                    for part in range(CORES):
                        start = pl.multiple_of(b * NJ + place_ref[which * CORES + part] * 8, 8)
                        out[slot, at, b, part * 8 : (part + 1) * 8, :] = total_ref[pl.ds(start, 8), :]


def product(pieces, at, high, low, got, place, k_local, tiles):
    rows, depth = high.shape
    width = tiles * LANES
    block = BLOCK
    b_local = rows // NJ
    ringed = len(pieces) == 2
    left = pl.BlockSpec((block, depth), lambda m, s: (m, 0))
    specs = [pl.BlockSpec(piece.shape, lambda m, s: (0, 0)) for piece in pieces]
    if ringed:
        specs[0] = pl.BlockSpec((Z, 1) + pieces[0].shape[2:], lambda m, s: (0, at, 0, 0))
    away = pl.BlockSpec((block * depth // LANES, LANES), lambda m, s: (m, 0))
    out = pl.BlockSpec((2, 2, block // NJ, 16, width), lambda m, s: (0, 0, m, 0, 0))
    shape = jax.ShapeDtypeStruct((2, 2, b_local, 16, width), jnp.float32)
    return pl.pallas_call(
        functools.partial(product_kernel, k_local, tiles, ringed),
        grid_spec=pltpu.PrefetchScalarGridSpec(
            num_scalar_prefetch=1,
            grid=(rows // block,),
            in_specs=specs + [left, left, away],
            out_specs=[out, out],
            scratch_shapes=[
                pltpu.VMEM((depth, width), jnp.bfloat16),
                pltpu.VMEM((depth, width), jnp.bfloat16),
                pltpu.VMEM((block, width), jnp.float32),
            ],
        ),
        out_shape=[shape, shape],
        compiler_params=pltpu.CompilerParams(vmem_limit_bytes=LIMIT2 * 1024 * 1024),
        cost_estimate=pl.CostEstimate(
            flops=rows * width, bytes_accessed=rows * width, transcendentals=0
        ),
    )(place, *pieces, high, low, got)


def per_device(amplitudes, integral, residual_in):
    row, col = lax.axis_index("row"), lax.axis_index("col")
    y, core, z, x = row // CORES, row % CORES, col // X, col % X
    k_local = O // lax.axis_size("row")
    c_local = amplitudes.shape[0]
    b_local = integral.shape[0] // NJ

    x_mate, x_other = mate(x, core), mate(x, 1 - core)
    xs = jnp.stack([x, x_other, x_mate, mate(x_mate, 1 - core)])
    zs = jnp.arange(Z)
    source = (zs[None, :, None] * X + xs[:, None, None]) * c_local + jnp.arange(c_local)[None, None, :]
    source = source.reshape(1, V).astype(jnp.int32)
    y_mate, y_other = mate(y, core), mate(y, 1 - core)
    ys = jnp.stack([y, y_other, y_mate, mate(y_mate, 1 - core)])
    place = (ys[:, None] * CORES + jnp.stack([core, 1 - core])[None, :]).reshape(8)
    place = jnp.concatenate([place, z[None]]).astype(jnp.int32)

    blocks, at = [], 0
    for tiles in PLAN:
        part = amplitudes.reshape(c_local * k_local, NI * V)[:, at * LANES : (at + tiles) * LANES]
        blocks.append(part.reshape(c_local * k_local * tiles, LANES))
        at += tiles
    lead, rest = blocks[0], blocks[1:]
    groups = [[q * X + r for q in range(Z)] for r in range(X)]
    gather = functools.partial(lax.all_gather, axis_name="col", axis=0, tiled=True, axis_index_groups=groups)
    gathered = gather(jnp.concatenate(rest)).reshape(Z, -1, LANES)
    pair = jnp.concatenate([lead, send(lead, to_x_other)])
    paired = gather(pair)
    half = V // 2
    packed = (ARRANGE * k_local * half // LANES, LANES)
    (away,) = arrange(away_kernel, integral, source[:, half:], k_local, [packed], jnp.float32)
    got = send(away, to_x_mate)
    natural = (ARRANGE, k_local * half)
    high, low = arrange(keep_kernel, integral, after(source[:, :half], away, pair), k_local, [natural] * 2, jnp.bfloat16)
    gathered = after(gathered, high)
    pieces, at = [], 0
    for block in rest:
        if pieces:
            gathered = after(gathered, outgoing)
        own = gathered[:, at : at + block.shape[0]]
        at += block.shape[0]
        outgoing = own.reshape(-1, LANES)
        pieces.append([own[:, None], send(outgoing, to_x_other)])
    pieces.append([paired])
    place = after(place, outgoing)
    plan = PLAN[1:] + PLAN[:1]

    count = len(plan)
    keeps, gives, firsts, halves, seconds = [], [], [], [], []
    for n in range(count + 3):
        if n < count:
            if n >= 2:
                place = after(place, firsts[n - 2])
            keep, give = product(pieces[n], 0, high, low, got, place, k_local, plan[n])
            place = after(place, keep)
            keeps.append(keep)
            gives.append(send(give, to_y_mate))
        if 0 <= n - 1 < count:
            mine = after(keeps[n - 1], keeps[n]) if n < count else keeps[n - 1]
            firsts.append(mine + gives[n - 1])
        if 0 <= n - 2 < count - LAST:
            halves.append(send(firsts[n - 2][1], to_y_other))
        if 0 <= n - 3 < count - LAST:
            mine = after(firsts[n - 3], keeps[n]) if n < count else firsts[n - 3]
            seconds.append(mine[0] + halves[n - 3])
    results = []
    for group in (seconds,):
        second = after(jnp.concatenate(group, axis=-1), keeps[-1])
        own, mates = second[0], second[1]
        total = own[:, :8] + send(own[:, 8:], to_core)
        total += send(mates[:, :8], to_x_mate)
        total += send(mates[:, 8:], to_x_mate_crossed)
        results.append(total)
    if LAST:
        (own, mates), (own_far, mates_far) = jnp.concatenate(firsts[-LAST:], axis=-1)
        total = own[:, :8]
        for value, target in (
            (own_far[:, :8], to_y_other),
            (own_far[:, 8:], to_y_other_crossed),
            (mates_far[:, :8], to_corner),
            (mates_far[:, 8:], to_corner_crossed),
            (mates[:, :8], to_x_mate),
            (mates[:, 8:], to_x_mate_crossed),
            (own[:, 8:], to_core),
        ):
            total += send(value, target)
        results.append(total)
    block = jnp.concatenate(results, axis=-1)
    first = PLAN[0] * LANES
    block = jnp.concatenate([block[..., -first:], block[..., :-first]], axis=-1)
    block = block.reshape(b_local, 8, NI, V).transpose(0, 2, 1, 3)
    return residual_in + block.reshape(residual_in.shape)


def solution(mesh):
    return jax.shard_map(
        per_device,
        mesh=mesh,
        in_specs=(P("col", "row"), P("col", "row"), P("col", "row")),
        out_specs=P("col", "row"),
        check_vma=False,
    )
```

```python
import functools

import jax
import jax.numpy as jnp
from jax import lax
from jax.experimental import pallas as pl
from jax.experimental.pallas import tpu as pltpu
from jax.sharding import PartitionSpec as P

O = 80
V = 320
NI = 4
NJ = 64
LANES = 128
X, Y, Z, CORES = 4, 4, 8, 2
PLAN = (2, 2, 2, 2, 2)

ARRANGE = 320
BLOCK = 320
LAST = 2
LIMIT1, LIMIT2 = 56, 32

dot = functools.partial(jnp.dot, preferred_element_type=jnp.float32)


def split(x):
    high = x.astype(jnp.bfloat16)
    return high, (x - high.astype(jnp.float32)).astype(jnp.bfloat16)


def mate(place, core):
    return (place + 1 - 2 * ((place + core) % 2)) % 4


def links(target):
    pairs = []
    for y in range(Y):
        for core in range(CORES):
            for z in range(Z):
                for x in range(X):
                    to_x, to_y, to_z, to_core = target(x, y, z, core)
                    here = ((y * CORES + core) * Z + z) * X + x
                    there = ((to_y * CORES + to_core) * Z + to_z % Z) * X + to_x
                    pairs.append((here, there))
    return pairs


def send(value, target):
    return lax.ppermute(value, ("row", "col"), links(target))


def to_x_mate(x, y, z, c):
    return mate(x, c), y, z, c


def to_x_mate_crossed(x, y, z, c):
    return mate(x, c), y, z, 1 - c


def to_x_other(x, y, z, c):
    return mate(x, 1 - c), y, z, c


def to_y_mate(x, y, z, c):
    return x, mate(y, c), z, c


def to_y_other(x, y, z, c):
    return x, mate(y, 1 - c), z, c


def to_y_other_crossed(x, y, z, c):
    return x, mate(y, 1 - c), z, 1 - c


def to_corner(x, y, z, c):
    return mate(x, c), mate(y, 1 - c), z, c


def to_corner_crossed(x, y, z, c):
    return mate(x, c), mate(y, 1 - c), z, 1 - c


def to_core(x, y, z, c):
    return x, y, z, 1 - c


def up(x, y, z, c):
    return x, y, z + 1, c


def down(x, y, z, c):
    return x, y, z - 1, c


def after(value, *others):
    return lax.optimization_barrier((value, *others))[0]


def turn(k_local, source_ref, left_ref):
    wanted = source_ref.shape[1]
    order = lax.broadcasted_iota(jnp.int32, (V, wanted), 0) == source_ref[...]
    rows = left_ref.shape[0]
    parts = [part[:, k * V : (k + 1) * V] for part in split(left_ref[...]) for k in range(k_local)]
    turned = dot(jnp.concatenate(parts, axis=0), order.astype(jnp.float32).astype(jnp.bfloat16))
    turned = [turned[n * rows : (n + 1) * rows] for n in range(2 * k_local)]
    return turned[:k_local], turned[k_local:]


def keep_kernel(k_local, source_ref, left_ref, high_ref, low_ref):
    high, low = turn(k_local, source_ref, left_ref)
    high_ref[...] = jnp.concatenate(high, axis=1).astype(jnp.bfloat16)
    low_ref[...] = jnp.concatenate(low, axis=1).astype(jnp.bfloat16)


def away_kernel(k_local, source_ref, left_ref, send_ref):
    rows = left_ref.shape[0]
    high, low = turn(k_local, source_ref, left_ref)
    away = jnp.concatenate([a + b for a, b in zip(high, low)], axis=1)
    full = away.shape[1] // LANES
    for t in range(full):
        send_ref[t * rows : (t + 1) * rows, :] = away[:, t * LANES : (t + 1) * LANES]
    rest = away[:, full * LANES :]
    send_ref[full * rows :, :] = jnp.concatenate([rest[: rows // 2], rest[rows // 2 :]], axis=1)


def arrange(kernel, left, source, k_local, blocks, dtype):
    rows, depth = left.shape
    block = ARRANGE
    return pl.pallas_call(
        functools.partial(kernel, k_local),
        grid=(rows // block,),
        in_specs=[pl.BlockSpec(source.shape, lambda m: (0, 0)), pl.BlockSpec((block, depth), lambda m: (m, 0))],
        out_specs=[pl.BlockSpec(shape, lambda m: (m, 0)) for shape in blocks],
        out_shape=[jax.ShapeDtypeStruct((shape[0] * (rows // block), shape[1]), dtype) for shape in blocks],
        compiler_params=pltpu.CompilerParams(vmem_limit_bytes=LIMIT1 * 1024 * 1024),
        cost_estimate=pl.CostEstimate(flops=rows * depth * V * 2, bytes_accessed=rows * depth * 6, transcendentals=0),
    )(source, left)


def product_kernel(k_local, tiles, ringed, raw, place_ref, *refs):
    *refs, right_high, right_low, total_ref = refs
    if raw:
        *pieces, high_ref, low_ref, got_ref, keep_ref, send_ref, got_high_ref, got_low_ref = refs
    else:
        *pieces, high_ref, low_ref, got_high_ref, got_low_ref, keep_ref, send_ref = refs
    shared = Z * O // 8
    size = O // 8 * k_local * tiles

    @pl.when(pl.program_id(0) == 0)
    def _():
        if ringed:
            own, other = pieces
            own, other = own.reshape(Z * size, LANES), other
            starts = ((own, 0, size), (other, 0, size))
        else:
            (rows_ref,) = pieces
            starts = ((rows_ref, 0, 2 * size), (rows_ref, size, 2 * size))
        for k in range(k_local):
            for t in range(tiles):
                for half, (ref, start, step) in enumerate(starts):
                    first = start + k * tiles + t
                    if step == size:
                        block = ref[pl.ds(first, shared, stride=k_local * tiles), :]
                    else:
                        block = jnp.concatenate(
                            [ref[pl.ds(first + z * step, O // 8, stride=k_local * tiles), :] for z in range(Z)]
                        )
                    high, low = split(block)
                    at = (2 * k + half) * shared
                    right_high[at : at + shared, t * LANES : (t + 1) * LANES] = high
                    right_low[at : at + shared, t * LANES : (t + 1) * LANES] = low

    rows, depth = high_ref.shape
    full = depth // LANES
    if raw:
        got = []
        for at in range(0, rows * depth // LANES, ARRANGE * depth // LANES):
            blocks = [got_ref[at + t * ARRANGE : at + (t + 1) * ARRANGE, :] for t in range(full)]
            rest = got_ref[at + full * ARRANGE : at + ARRANGE * depth // LANES, :]
            blocks.append(jnp.concatenate([rest[:, : LANES // 2], rest[:, LANES // 2 :]], axis=0))
            got.append(jnp.concatenate(blocks, axis=1))
        got_high, got_low = split(jnp.concatenate(got, axis=0))
        got_high_ref[...] = got_high
        got_low_ref[...] = got_low
    else:
        got_high, got_low = got_high_ref[...], got_low_ref[...]
    high = jnp.concatenate([high_ref[...], got_high], axis=0)
    low = jnp.concatenate([low_ref[...], got_low], axis=0)
    total_ref[...] = dot(high, right_high[...]) + dot(high, right_low[...]) + dot(low, right_high[...])
    for at in range(2):
        for b in range(rows // NJ):
            for out, slots in ((keep_ref, (0, 1)), (send_ref, (2, 3))):
                for slot, which in enumerate(slots):
                    for part in range(CORES):
                        start = pl.multiple_of(at * rows + b * NJ + place_ref[which * CORES + part] * 8, 8)
                        out[slot, at, b, part * 8 : (part + 1) * 8, :] = total_ref[pl.ds(start, 8), :]


def product(pieces, at, high, low, got, place, k_local, tiles):
    raw = len(got) == 1
    rows, depth = high.shape
    width = tiles * LANES
    block = BLOCK
    b_local = rows // NJ
    ringed = len(pieces) == 2
    left = pl.BlockSpec((block, depth), lambda m, s: (m, 0))
    specs = [pl.BlockSpec(piece.shape, lambda m, s: (0, 0)) for piece in pieces]
    if ringed:
        specs[0] = pl.BlockSpec((Z, 1) + pieces[0].shape[2:], lambda m, s: (0, at, 0, 0))
    away = pl.BlockSpec((block * depth // LANES, LANES), lambda m, s: (m, 0))
    out = pl.BlockSpec((2, 2, block // NJ, 16, width), lambda m, s: (0, 0, m, 0, 0))
    shape = jax.ShapeDtypeStruct((2, 2, b_local, 16, width), jnp.float32)
    return pl.pallas_call(
        functools.partial(product_kernel, k_local, tiles, ringed, raw),
        grid_spec=pltpu.PrefetchScalarGridSpec(
            num_scalar_prefetch=1,
            grid=(rows // block,),
            in_specs=specs + [left, left] + ([away] if raw else [left, left]),
            out_specs=[out, out] + ([left, left] if raw else []),
            scratch_shapes=[
                pltpu.VMEM((depth, width), jnp.bfloat16),
                pltpu.VMEM((depth, width), jnp.bfloat16),
                pltpu.VMEM((2 * block, width), jnp.float32),
            ],
        ),
        out_shape=[shape, shape] + ([jax.ShapeDtypeStruct(high.shape, high.dtype)] * 2 if raw else []),
        compiler_params=pltpu.CompilerParams(vmem_limit_bytes=(LIMIT2 if ringed else LIMIT1) * 1024 * 1024),
        cost_estimate=pl.CostEstimate(
            flops=rows * width, bytes_accessed=rows * width, transcendentals=0
        ),
    )(place, *pieces, high, low, *got)


def per_device(amplitudes, integral, residual_in):
    row, col = lax.axis_index("row"), lax.axis_index("col")
    y, core, z, x = row // CORES, row % CORES, col // X, col % X
    k_local = O // lax.axis_size("row")
    c_local = amplitudes.shape[0]
    b_local = integral.shape[0] // NJ

    x_mate, x_other = mate(x, core), mate(x, 1 - core)
    xs = jnp.stack([x, x_other, x_mate, mate(x_mate, 1 - core)])
    zs = jnp.arange(Z)
    source = (zs[None, :, None] * X + xs[:, None, None]) * c_local + jnp.arange(c_local)[None, None, :]
    source = source.reshape(1, V).astype(jnp.int32)
    y_mate, y_other = mate(y, core), mate(y, 1 - core)
    ys = jnp.stack([y, y_other, y_mate, mate(y_mate, 1 - core)])
    place = (ys[:, None] * CORES + jnp.stack([core, 1 - core])[None, :]).reshape(8)
    place = jnp.concatenate([place, z[None]]).astype(jnp.int32)

    blocks, at = [], 0
    for tiles in PLAN:
        part = amplitudes.reshape(c_local * k_local, NI * V)[:, at * LANES : (at + tiles) * LANES]
        blocks.append(part.reshape(c_local * k_local * tiles, LANES))
        at += tiles
    lead, rest = blocks[0], blocks[1:]
    groups = [[q * X + r for q in range(Z)] for r in range(X)]
    gather = functools.partial(lax.all_gather, axis_name="col", axis=0, tiled=True, axis_index_groups=groups)
    gathered = gather(jnp.concatenate(rest)).reshape(Z, -1, LANES)
    pair = jnp.concatenate([lead, send(lead, to_x_other)])
    paired = gather(pair)
    half = V // 2
    packed = (ARRANGE * k_local * half // LANES, LANES)
    (away,) = arrange(away_kernel, integral, source[:, half:], k_local, [packed], jnp.float32)
    got = [send(away, to_x_mate)]
    natural = (ARRANGE, k_local * half)
    high, low = arrange(keep_kernel, integral, after(source[:, :half], away, pair), k_local, [natural] * 2, jnp.bfloat16)
    gathered = after(gathered, high)
    pieces, at = [], 0
    for block in rest:
        if pieces:
            gathered = after(gathered, outgoing)
        own = gathered[:, at : at + block.shape[0]]
        at += block.shape[0]
        outgoing = own.reshape(-1, LANES)
        pieces.append([own[:, None], send(outgoing, to_x_other)])
    pieces.append([paired])
    place = after(place, outgoing)
    plan = PLAN[1:] + PLAN[:1]

    count = len(plan)
    keeps, gives, firsts, halves, seconds = [], [], [], [], []
    for n in range(count + 3):
        if n < count:
            if n >= 2:
                place = after(place, firsts[n - 2])
            keep, give, *parts = product(pieces[n], 0, high, low, got, place, k_local, plan[n])
            got = parts or got
            place = after(place, keep)
            keeps.append(keep)
            gives.append(send(give, to_y_mate))
        if 0 <= n - 1 < count:
            mine = after(keeps[n - 1], keeps[n]) if n < count else keeps[n - 1]
            firsts.append(mine + gives[n - 1])
        if 0 <= n - 2 < count - LAST:
            halves.append(send(firsts[n - 2][1], to_y_other))
        if 0 <= n - 3 < count - LAST:
            mine = after(firsts[n - 3], keeps[n]) if n < count else firsts[n - 3]
            seconds.append(mine[0] + halves[n - 3])
    results = []
    for group in (seconds,):
        second = after(jnp.concatenate(group, axis=-1), keeps[-1])
        own, mates = second[0], second[1]
        total = own[:, :8] + send(own[:, 8:], to_core)
        total += send(mates[:, :8], to_x_mate)
        total += send(mates[:, 8:], to_x_mate_crossed)
        results.append(total)
    if LAST:
        (own, mates), (own_far, mates_far) = jnp.concatenate(firsts[-LAST:], axis=-1)
        total = own[:, :8]
        for value, target in (
            (own_far[:, :8], to_y_other),
            (own_far[:, 8:], to_y_other_crossed),
            (mates_far[:, :8], to_corner),
            (mates_far[:, 8:], to_corner_crossed),
            (mates[:, :8], to_x_mate),
            (mates[:, 8:], to_x_mate_crossed),
            (own[:, 8:], to_core),
        ):
            total += send(value, target)
        results.append(total)
    block = jnp.concatenate(results, axis=-1)
    first = PLAN[0] * LANES
    block = jnp.concatenate([block[..., -first:], block[..., :-first]], axis=-1)
    block = block.reshape(b_local, 8, NI, V).transpose(0, 2, 1, 3)
    return residual_in + block.reshape(residual_in.shape)


def solution(mesh):
    return jax.shard_map(
        per_device,
        mesh=mesh,
        in_specs=(P("col", "row"), P("col", "row"), P("col", "row")),
        out_specs=P("col", "row"),
        check_vma=False,
    )
```
